32 devices in a mesh: groups: 2 (over y), replica: 8 (over z, x), tensor: 2 (over core).
Axes of the slice: x: 2, y: 2, z: 4, core: 2. Of those that a mesh axis runs over, the one named last changes fastest.
Arguments:
- hidden: bfloat16 [4, 512, 8192], P(None, ('groups', 'replica'), 'tensor'), parts along dimension 1, may hold values from -6 to 6
- down_weight: bfloat16 [16, 64, 8192], P('replica', None, 'tensor'), may hold values from -0.0625 to 0.0625
- up_weight: bfloat16 [16, 64, 8192], P('replica', None, 'tensor'), may hold values from -0.75 to 0.75
- adapter_update_scale: float32 [16], replicated, may hold values from 0.5 to 2
- input_norm_weight: float32 [8192], P('tensor'), may hold values from 0.75 to 1.3
- segment_length: int32 [32], P('groups'), parts along dimension 0, may hold values from 8 to 16, as said below
- moves: int32 [8, 3], P('groups'), parts along dimension 0, may hold values from 0 to 7, as said below
Outputs:
- served: bfloat16 [4, 768, 8192], P(None, ('groups', 'replica'), 'tensor'), parts along dimension 1
The draws below stay inside these ranges and needn't reach their ends.
There are 2 independent parts, one for each index of `groups`. The reference program is written for one: setup_inputs(seed, part) draws one part's arguments, and reference() takes and returns one part's arrays. A program takes and returns all parts, laid end to end along the dimension named above; an argument that names none is the same for every part. Nothing has to cross between parts.
Inputs may be any that keep to these rules, and one draw needn't show every extreme that they name: `moves`: column 0 names 4 different source replicas and column 2 names 4 different target replicas, none of which is a source; column 1 is below 2. `segment_length`: every segment named by moves has 16 live requests.
All inputs are finite; a program needn't handle non-finite values.
Results may differ from the reference program's by a relative error of at most 0.0057.
Values may be sent and summed in bfloat16 or wider, within the bound.
No kernel may reach another device: no remote copies, remote signals or barrier semaphores. Data moves between devices by JAX's collectives and lax.ppermute only.
A program may use at most 64 MiB of HBM per device.

```python
import math
import jax
import jax.numpy as jnp
from jax import lax

MODEL_WIDTH = 8192
ADAPTER_RANK = 64
SEG = 16
ADP_DEV = 2
MOVES = 4
STEPS = 4
REPLICAS = 8
ADAPTER_TOTAL = 16
ROWS = 256


def migration_plan(key):
    order_key, slot_key = jax.random.split(key)
    order = jax.random.permutation(order_key, REPLICAS).astype(jnp.int32)
    chosen_slots = jax.random.randint(slot_key, (MOVES,), 0, ADP_DEV).astype(jnp.int32)
    return (order[:MOVES], chosen_slots, order[MOVES:2 * MOVES])


def draw_moves(key, part):
    sources, chosen_slots, targets = migration_plan(key)
    return jnp.stack([sources, chosen_slots, targets], axis=1).astype(jnp.int32)


def draw_segment_length(key, part):
    sources, chosen_slots, targets = migration_plan(key)
    key = jax.random.fold_in(key, 11)
    counts = jax.random.randint(key, (ADAPTER_TOTAL,), SEG // 2, SEG + 1).astype(jnp.int32)
    moved = sources * ADP_DEV + chosen_slots
    busy = jnp.any(jnp.arange(ADAPTER_TOTAL, dtype=jnp.int32)[:, None] == moved[None, :], axis=1)
    return jnp.where(busy, SEG, counts).astype(jnp.int32)


def draw_input_norm_weight(key, part):
    key = jax.random.fold_in(key, 37)
    values = jax.random.uniform(key, (MODEL_WIDTH,), jnp.float32, 0.0, 1.0)
    return (0.75 + 0.55 * values).astype(jnp.float32)


def levels(own_key, shape, pieces, least, top_value):
    def one(axis_at, shards_of):
        steps = jax.random.uniform(jax.random.fold_in(jax.random.fold_in(own_key, 6), axis_at), (shards_of,), jnp.float32, least / len(pieces), top_value / len(pieces))
        return jnp.repeat(jnp.exp(steps), shape[axis_at] // shards_of).reshape((-1,) + (1,) * (len(shape) - axis_at - 1))

    gain = one(*pieces[0])
    for cut in pieces[1:]:
        gain = gain * one(*cut)
    return gain


def normal_values(key, shape, scale, reach, pieces=(), held_as=jnp.bfloat16):
    factor_of = levels(key, shape, pieces, -0.22, 0.18) if pieces else 1.0
    drawn = jax.random.normal(key, shape, jnp.float32) * scale * factor_of
    return jnp.minimum(jnp.maximum(drawn, -reach), reach).astype(held_as)


def setup_inputs(seed: int = 0, part: int = 0) -> dict:
    seeds = jax.random.split(jax.random.key(seed), 8)
    part_keys = jax.random.split(jax.random.fold_in(seeds[7], part), 8)
    return {
        "hidden": normal_values(part_keys[0], (STEPS, ROWS, MODEL_WIDTH), 1.0, 6.0, ((1, 8), (2, 2))),
        "down_weight": normal_values(seeds[1], (ADAPTER_TOTAL, ADAPTER_RANK, MODEL_WIDTH), MODEL_WIDTH ** -0.5, 0.0625, ((0, 8), (2, 2))),
        "up_weight": normal_values(seeds[2], (ADAPTER_TOTAL, ADAPTER_RANK, MODEL_WIDTH), ADAPTER_RANK ** -0.5, 0.75, ((0, 8), (2, 2))),
        "adapter_update_scale": jnp.clip(jnp.exp(jax.random.uniform(seeds[3], (ADAPTER_TOTAL,), jnp.float32, math.log(0.5), math.log(2.0))), 0.5, 2.0),
        "input_norm_weight": draw_input_norm_weight(jax.random.fold_in(seeds[7], 71), part),
        "segment_length": draw_segment_length(jax.random.fold_in(jax.random.fold_in(seeds[7], part), 71), part),
        "moves": draw_moves(jax.random.fold_in(jax.random.fold_in(seeds[7], part), 71), part),
    }


epsilon = 1e-05

def apply_lowrank_updates(request_rows, shrink_weights, expand_weights, scales, input_norm_weight):
    values = request_rows.astype(jnp.float32)
    squares = lax.optimization_barrier(jnp.sum(values * values, axis=3, keepdims=True))
    normed = (values * lax.rsqrt(squares / MODEL_WIDTH + epsilon) * input_norm_weight).astype(jnp.bfloat16)
    shrink = jnp.einsum('tnsd,nrd->tnsr', normed.astype(jnp.float32), shrink_weights.astype(jnp.float32))
    rounded = lax.optimization_barrier(shrink.astype(jnp.bfloat16)).astype(jnp.float32)
    delta = jnp.einsum('tnsr,nrd->tnsd', rounded, expand_weights.astype(jnp.float32))
    return (delta * scales[None, :, None, None]).astype(jnp.bfloat16)

def reference(hidden, down_weight, up_weight, adapter_update_scale, input_norm_weight, segment_length, moves):
    segments = hidden.reshape(STEPS, ADAPTER_TOTAL, SEG, MODEL_WIDTH)
    alive = jnp.arange(SEG, dtype=jnp.int32)[None, :] < segment_length[:, None]
    segments = jnp.where(alive[None, :, :, None], segments, jnp.zeros((), jnp.bfloat16))
    moved = (moves[:, 0] * ADP_DEV + moves[:, 1]).astype(jnp.int32)
    adapter_numbers = jnp.arange(ADAPTER_TOTAL, dtype=jnp.int32)
    departed = jnp.any(adapter_numbers[:, None] == moved[None, :], axis=1)
    resident_table = jnp.where(departed, -1, adapter_numbers).astype(jnp.int32).reshape(REPLICAS, ADP_DEV)
    replica_numbers = jnp.arange(REPLICAS, dtype=jnp.int32)
    matched = moves[:, 2][None, :] == replica_numbers[:, None]
    guest_found = lax.optimization_barrier(jnp.sum(jnp.where(matched, moved[None, :], 0), axis=1)).astype(jnp.int32)
    guest_table = jnp.where(jnp.any(matched, axis=1), guest_found, -1).astype(jnp.int32)
    table = jnp.concatenate([resident_table, guest_table[:, None]], axis=1)

    def serve(entries):
        present = entries >= 0
        picked_adapter = jnp.maximum(entries, 0).astype(jnp.int32)
        request_rows = jnp.where(present[None, :, None, None], segments[:, picked_adapter], jnp.zeros((), jnp.bfloat16))
        return apply_lowrank_updates(request_rows, down_weight[picked_adapter], up_weight[picked_adapter], adapter_update_scale[picked_adapter], input_norm_weight)
    result = lax.map(serve, table)
    return jnp.transpose(result, (1, 0, 2, 3, 4)).reshape(STEPS, REPLICAS * (ADP_DEV + 1) * SEG, MODEL_WIDTH)
```

```python
import functools

import jax
import jax.numpy as jnp
from jax import lax
from jax.experimental import pallas as pl
from jax.experimental.pallas import tpu as pltpu
from jax.sharding import PartitionSpec as P

MODEL_WIDTH = 8192
MOVES = 4
EPSILON = 1e-05
ROW_BLOCK = 16
VMEM_LIMIT = 48 * 1024 * 1024

SMEM = pl.BlockSpec(memory_space=pltpu.SMEM)
VMEM = pl.BlockSpec(memory_space=pltpu.VMEM)
ANY = pl.BlockSpec(memory_space=pl.ANY)
F32 = jnp.float32
BF16 = jnp.bfloat16


def params():
    return pltpu.CompilerParams(vmem_limit_bytes=VMEM_LIMIT)


def leaving_slot(moves, me):
    slot, sending = jnp.int32(0), jnp.int32(0)
    for move in range(MOVES):
        here = moves[move, 0] == me
        slot = jnp.where(here, moves[move, 1], slot)
        sending = jnp.where(here, 1, sending)
    return slot, sending


def source_of(moves, target, otherwise):
    source = otherwise
    for move in range(MOVES):
        source = jnp.where(moves[move, 2] == target, moves[move, 0], source)
    return source


def piece_place(index, blocks):
    return index % blocks, index // blocks


def cut_kernel(pieces, width, me_ref, moves, up, *refs):
    outs, sems = refs[:pieces], refs[pieces]
    slot, _ = leaving_slot(moves, me_ref[0])
    blocks = up.shape[1] // ROW_BLOCK
    copies = []
    for index in range(pieces):
        rows, columns = piece_place(index, blocks)
        copies.append(
            pltpu.make_async_copy(
                up.at[slot, pl.ds(rows * ROW_BLOCK, ROW_BLOCK), pl.ds(columns * width, width)],
                outs[index],
                sems.at[index],
            )
        )
    for copy in copies:
        copy.start()
    for copy in copies:
        copy.wait()


def project_kernel(hidden, down, gain, out):
    adapters, rank, width = down.shape
    steps = hidden.shape[0]
    chunk = 512
    for n in range(adapters):
        total = jnp.zeros((steps * ROW_BLOCK, rank), F32)
        squares = jnp.zeros((steps * ROW_BLOCK, 1), F32)
        for c in range(0, width, chunk):
            values = hidden[:, n * ROW_BLOCK : (n + 1) * ROW_BLOCK, c : c + chunk]
            values = values.reshape(steps * ROW_BLOCK, chunk).astype(F32)
            squares += jnp.sum(values * values, axis=1, keepdims=True)
            gained = values * gain[:, c : c + chunk]
            high = gained.astype(BF16)
            low = (gained - high.astype(F32)).astype(BF16)
            weights = down[n, :, c : c + chunk]
            for part in (high, low):
                total += lax.dot_general(
                    part, weights, (((1,), (1,)), ((), ())), preferred_element_type=F32
                )
        out[n] = jnp.concatenate(
            [total, jnp.broadcast_to(squares, (steps * ROW_BLOCK, rank))], axis=1
        )


def shrink_kernel(rank, me_ref, moves, lengths, mine, other, kept, rider):
    me = me_ref[0]
    slot, sending = leaving_slot(moves, me)
    adapters, rows, _ = mine.shape
    leaving = None
    for n in range(adapters):
        total = mine[n] + other[n]
        squares = total[:, rank : rank + 1]
        shrink = total[:, :rank] * lax.rsqrt(squares / MODEL_WIDTH + EPSILON)
        place = lax.broadcasted_iota(jnp.int32, (rows, rank), 0) % ROW_BLOCK
        shrink = jnp.where(place < lengths[me * adapters + n], shrink, 0.0)
        leaving = shrink if n == 0 else jnp.where(slot == n, shrink, leaving)
        removed = (sending == 1) & (slot == n)
        kept[n] = jnp.where(removed, 0.0, shrink).astype(BF16)
    leaving = leaving.astype(BF16)
    for t in range(rows // ROW_BLOCK):
        rider[:, t * rank : (t + 1) * rank] = leaving[t * ROW_BLOCK : (t + 1) * ROW_BLOCK]


def resident_kernel(me_ref, scales, kept, up, out, held, sem):
    adapters, rank, width = up.shape
    steps = held.shape[0]
    chunk = 1024
    for n in range(adapters):
        scale = scales[me_ref[0] * adapters + n]
        for c in range(0, width, chunk):
            delta = jnp.dot(kept[n], up[n, :, c : c + chunk], preferred_element_type=F32)
            held[:, n * ROW_BLOCK : (n + 1) * ROW_BLOCK, c : c + chunk] = (
                (delta * scale).astype(BF16).reshape(steps, ROW_BLOCK, chunk)
            )
    copy = pltpu.make_async_copy(held, out.at[:, : adapters * ROW_BLOCK, :], sem)
    copy.start()
    copy.wait()


def regroup_kernel(pieces, width, me_ref, moves, rider, *refs):
    arrived, outs = refs[:pieces], refs[pieces : 2 * pieces]
    held, sems = refs[2 * pieces :]
    me = me_ref[0]
    copies = [
        pltpu.make_async_copy(arrived[m], held.at[m], sems.at[m]) for m in range(pieces)
    ]
    for copy in copies:
        copy.start()
    for m in range(pieces):
        outs[m][:, width:] = rider[...]
    for copy in copies:
        copy.wait()
    for m in range(pieces):
        target = me ^ m
        outs[m][:, :width] = held[source_of(moves, target, target) ^ me]


def guest_kernel(pieces, width, me_ref, moves, scales, *refs):
    arrived = refs[:pieces]
    out = refs[pieces + 1]
    weights, rider, held, sems, rider_sem = refs[pieces + 2 :]
    me = me_ref[0]
    rank, full = weights.shape
    steps = held.shape[0]
    adapters = out.shape[1] // ROW_BLOCK - 1
    source = source_of(moves, me, me)
    visited = source != me
    slot, _ = leaving_slot(moves, source)
    scale = scales[source * adapters + slot]
    blocks = rank // ROW_BLOCK
    copies = []
    for m in range(pieces):
        rows, columns = piece_place(source ^ me ^ m, blocks)
        copies.append(
            pltpu.make_async_copy(
                arrived[m].at[:, pl.ds(0, width)],
                weights.at[
                    pl.ds(pl.multiple_of(rows * ROW_BLOCK, ROW_BLOCK), ROW_BLOCK),
                    pl.ds(pl.multiple_of(columns * width, 128), width),
                ],
                sems.at[m],
            )
        )
    for copy in copies:
        copy.start()
    size = rider.shape[1]
    for m in range(pieces):

        @pl.when((source ^ me) == m)
        def _():
            copy = pltpu.make_async_copy(
                arrived[m].at[:, pl.ds(width, size)], rider, rider_sem
            )
            copy.start()
            copy.wait()

    for copy in copies:
        copy.wait()
    shrink = jnp.concatenate(
        [rider[:, t * rank : (t + 1) * rank] for t in range(steps)], axis=0
    )
    chunk = 1024
    for c in range(0, full, chunk):
        delta = jnp.dot(shrink, weights[:, c : c + chunk], preferred_element_type=F32)
        delta = jnp.where(visited, delta * scale, 0.0)
        held[:, :, c : c + chunk] = delta.astype(BF16).reshape(steps, ROW_BLOCK, chunk)
    copy = pltpu.make_async_copy(
        held, out.at[:, pl.ds(adapters * ROW_BLOCK, ROW_BLOCK), :], rider_sem
    )
    copy.start()
    copy.wait()


def exchange(parts, replicas):
    done = [parts[0]] + [None] * (replicas - 1)
    for m in sorted(range(1, replicas), reverse=True):
        done[m] = lax.ppermute(parts[m], "replica", [(i, i ^ m) for i in range(replicas)])
    return done


def scattered(
    replicas, hidden, down_weight, up_weight, scales, gain, lengths, moves
):
    adapters, rank, width = down_weight.shape
    steps = hidden.shape[0]
    rows = steps * ROW_BLOCK
    piece = rank * width // (replicas * ROW_BLOCK)
    ride = rank * steps
    me = lax.axis_index("replica").astype(jnp.int32).reshape(1)
    shape = jax.ShapeDtypeStruct

    parts = pl.pallas_call(
        functools.partial(cut_kernel, replicas, piece),
        out_shape=[shape((ROW_BLOCK, piece), BF16)] * replicas,
        in_specs=[SMEM, SMEM, ANY],
        out_specs=[ANY] * replicas,
        scratch_shapes=[pltpu.SemaphoreType.DMA((replicas,))],
        compiler_params=params(),
        cost_estimate=pl.CostEstimate(
            flops=0, bytes_accessed=2 * rank * width * 2, transcendentals=0
        ),
        name="cut",
    )(me, moves, up_weight)
    parts = exchange(parts, replicas)

    mine = pl.pallas_call(
        project_kernel,
        out_shape=shape((adapters, rows, 2 * rank), F32),
        in_specs=[VMEM] * 3,
        out_specs=VMEM,
        compiler_params=params(),
        cost_estimate=pl.CostEstimate(
            flops=4 * adapters * rows * rank * width,
            bytes_accessed=4 * adapters * rows * width,
            transcendentals=0,
        ),
        name="project",
    )(hidden, down_weight, gain.reshape(1, width))
    other = lax.ppermute(mine, "tensor", [(0, 1), (1, 0)])
    kept, rider = pl.pallas_call(
        functools.partial(shrink_kernel, rank),
        out_shape=[shape((adapters, rows, rank), BF16), shape((ROW_BLOCK, ride), BF16)],
        in_specs=[SMEM, SMEM, SMEM, VMEM, VMEM],
        out_specs=[VMEM, VMEM],
        compiler_params=params(),
        name="shrink",
    )(me, moves, lengths, mine, other)
    out_shape = shape((steps, (adapters + 1) * ROW_BLOCK, width), BF16)
    out = pl.pallas_call(
        resident_kernel,
        out_shape=out_shape,
        in_specs=[SMEM, SMEM, VMEM, VMEM],
        out_specs=ANY,
        scratch_shapes=[
            pltpu.VMEM((steps, adapters * ROW_BLOCK, width), BF16),
            pltpu.SemaphoreType.DMA,
        ],
        compiler_params=params(),
        cost_estimate=pl.CostEstimate(
            flops=2 * adapters * rows * rank * width,
            bytes_accessed=4 * adapters * rows * width,
            transcendentals=0,
        ),
        name="resident",
    )(me, scales, kept, up_weight)

    parts = pl.pallas_call(
        functools.partial(regroup_kernel, replicas, piece),
        out_shape=[shape((ROW_BLOCK, piece + ride), BF16)] * replicas,
        in_specs=[SMEM, SMEM, VMEM] + [ANY] * replicas,
        out_specs=[VMEM] * replicas,
        scratch_shapes=[
            pltpu.VMEM((replicas, ROW_BLOCK, piece), BF16),
            pltpu.SemaphoreType.DMA((replicas,)),
        ],
        compiler_params=params(),
        cost_estimate=pl.CostEstimate(
            flops=0, bytes_accessed=2 * rank * width * 2, transcendentals=0
        ),
        name="regroup",
    )(me, moves, rider, *parts)
    parts = exchange(parts, replicas)

    return pl.pallas_call(
        functools.partial(guest_kernel, replicas, piece),
        out_shape=out_shape,
        in_specs=[SMEM, SMEM, SMEM] + [ANY] * (replicas + 1),
        out_specs=ANY,
        scratch_shapes=[
            pltpu.VMEM((rank, width), BF16),
            pltpu.VMEM((ROW_BLOCK, ride), BF16),
            pltpu.VMEM((steps, ROW_BLOCK, width), BF16),
            pltpu.SemaphoreType.DMA((replicas,)),
            pltpu.SemaphoreType.DMA,
        ],
        input_output_aliases={3 + replicas: 0},
        compiler_params=params(),
        cost_estimate=pl.CostEstimate(
            flops=2 * rows * rank * width,
            bytes_accessed=2 * (rank + rows) * width,
            transcendentals=0,
        ),
        name="guest",
    )(me, moves, scales, *parts, out)


def summed(hidden, down_weight, up_weight, scales, gain, lengths, moves):
    adapters, rank, width = down_weight.shape
    steps = hidden.shape[0]
    segment = hidden.shape[1] // adapters
    me = lax.axis_index("replica")
    first = me * adapters
    sources, slots, targets = moves[:, 0], moves[:, 1], moves[:, 2]
    here = lax.dynamic_slice_in_dim(lengths, first, adapters)
    alive = jnp.arange(segment, dtype=jnp.int32)[None, :] < here[:, None]
    values = jnp.where(
        alive[None, :, :, None], hidden.reshape(steps, adapters, segment, width), 0
    ).astype(F32)
    squares = lax.psum(jnp.sum(values * values, axis=3), "tensor")
    normed = (values * lax.rsqrt(squares[..., None] / MODEL_WIDTH + EPSILON) * gain).astype(BF16)
    shrink = jnp.einsum("tnsd,nrd->tnsr", normed, down_weight, preferred_element_type=F32)
    shrink = lax.psum(shrink, "tensor").astype(BF16)
    delta = jnp.einsum("tnsr,nrd->tnsd", shrink, up_weight, preferred_element_type=F32)
    scale = lax.dynamic_slice_in_dim(scales, first, adapters)
    served = (delta * scale[None, :, None, None]).astype(BF16)
    leaving = sources == me
    slot = jnp.sum(jnp.where(leaving, slots, 0))
    parcel = lax.dynamic_index_in_dim(served, slot, 1, keepdims=False)
    guest = jnp.zeros_like(parcel)
    for move in range(MOVES):
        arrived = lax.psum(jnp.where(leaving[move], parcel, jnp.zeros_like(parcel)), "replica")
        guest = jnp.where(targets[move] == me, arrived, guest)
    removed = (jnp.arange(adapters) == slot) & jnp.any(leaving)
    served = jnp.where(removed[None, :, None, None], jnp.zeros_like(served), served)
    result = jnp.concatenate([served, guest[:, None]], axis=1)
    return result.reshape(steps, (adapters + 1) * segment, width)


def solution(mesh):
    replicas = mesh.shape["replica"]
    body = functools.partial(scattered, replicas) if replicas == 8 else summed
    return jax.shard_map(
        body,
        mesh=mesh,
        in_specs=(
            P(None, ("groups", "replica"), "tensor"),
            P("replica", None, "tensor"),
            P("replica", None, "tensor"),
            P(),
            P("tensor"),
            P("groups"),
            P("groups", None),
        ),
        out_specs=P(None, ("groups", "replica"), "tensor"),
        check_vma=False,
    )
```

```python
import functools

import jax
import jax.numpy as jnp
from jax import lax
from jax.experimental import pallas as pl
from jax.experimental.pallas import tpu as pltpu
from jax.sharding import PartitionSpec as P

MODEL_WIDTH = 8192
MOVES = 4
EPSILON = 1e-05
ROW_BLOCK = 16
VMEM_LIMIT = 48 * 1024 * 1024

SMEM = pl.BlockSpec(memory_space=pltpu.SMEM)
VMEM = pl.BlockSpec(memory_space=pltpu.VMEM)
ANY = pl.BlockSpec(memory_space=pl.ANY)
F32 = jnp.float32
BF16 = jnp.bfloat16


def params():
    return pltpu.CompilerParams(vmem_limit_bytes=VMEM_LIMIT)


def scalar_rows(moves, column, value, pick, otherwise):
    found = otherwise
    for move in range(MOVES):
        found = jnp.where(moves[move, column] == value, moves[move, pick], found)
    return found


PARTNER, LEAVING, SOURCE, SOURCE_SLOT = range(4)


def cut_kernel(moves, up, plan, out, sem):
    me = lax.axis_index("replica")
    nothing = jnp.int32(-1)
    leaving = scalar_rows(moves, 0, me, 1, nothing)
    copy = pltpu.make_async_copy(up.at[jnp.maximum(leaving, 0)], out, sem)
    copy.start()
    source = scalar_rows(moves, 2, me, 0, nothing)
    target = scalar_rows(moves, 0, me, 2, nothing)
    plan[PARTNER] = me ^ jnp.where(leaving >= 0, target, source)
    plan[LEAVING] = leaving
    plan[SOURCE] = source
    plan[SOURCE_SLOT] = scalar_rows(moves, 2, me, 1, nothing)
    copy.wait()


def project_kernel(hidden, down, gain, out):
    adapters, rank, width = down.shape
    steps = hidden.shape[0]
    chunk = 512
    for n in range(adapters):
        total = jnp.zeros((steps * ROW_BLOCK, rank), F32)
        squares = jnp.zeros((steps * ROW_BLOCK, 1), F32)
        for c in range(0, width, chunk):
            values = hidden[:, n * ROW_BLOCK : (n + 1) * ROW_BLOCK, c : c + chunk]
            values = values.reshape(steps * ROW_BLOCK, chunk).astype(F32)
            squares += jnp.sum(values * values, axis=1, keepdims=True)
            gained = values * gain[:, c : c + chunk]
            high = gained.astype(BF16)
            low = (gained - high.astype(F32)).astype(BF16)
            weights = down[n, :, c : c + chunk]
            for part in (high, low):
                total += lax.dot_general(
                    part, weights, (((1,), (1,)), ((), ())), preferred_element_type=F32
                )
        out[n] = jnp.concatenate(
            [total, jnp.broadcast_to(squares, (steps * ROW_BLOCK, rank))], axis=1
        )


def shrink_kernel(plan, lengths, mine, other, kept, leaving_out):
    first = lax.axis_index("replica") * mine.shape[0]
    adapters, rows, lanes = mine.shape
    rank = lanes // 2
    leaving = None
    for n in range(adapters):
        total = mine[n] + other[n]
        squares = total[:, rank : rank + 1]
        shrink = total[:, :rank] * lax.rsqrt(squares / MODEL_WIDTH + EPSILON)
        place = lax.broadcasted_iota(jnp.int32, (rows, rank), 0) % ROW_BLOCK
        shrink = jnp.where(place < lengths[first + n], shrink, 0.0)
        removed = plan[LEAVING] == n
        leaving = shrink if n == 0 else jnp.where(removed, shrink, leaving)
        kept[n] = jnp.where(removed, 0.0, shrink).astype(BF16)
    leaving_out[...] = leaving.astype(BF16)


def serve(shrink, weights, scale, held, row, out, sems):
    width = weights.shape[-1]
    steps = held.shape[0]
    chunk = 1024
    copies = []
    for k, c in enumerate(range(0, width, chunk)):
        delta = jnp.dot(shrink, weights[:, c : c + chunk], preferred_element_type=F32)
        held[:, :, c : c + chunk] = (
            (delta * scale).astype(BF16).reshape(steps, ROW_BLOCK, chunk)
        )
        copy = pltpu.make_async_copy(
            held.at[:, :, c : c + chunk],
            out.at[:, pl.ds(row, ROW_BLOCK), c : c + chunk],
            sems.at[k],
        )
        copy.start()
        copies.append(copy)
    return copies


def resident_kernel(scales, kept, up, out, held, sems):
    first = lax.axis_index("replica") * up.shape[0]
    copies = []
    for n in range(up.shape[0]):
        copies += serve(
            kept[n], up.at[n], scales[first + n], held.at[n], n * ROW_BLOCK, out, sems.at[n]
        )
    for copy in copies:
        copy.wait()


def guest_kernel(plan, scales, weights, shrink, _, out, held, sems):
    adapters = out.shape[1] // ROW_BLOCK - 1
    visited = plan[SOURCE] >= 0

    @pl.when(visited)
    def _():
        scale = scales[plan[SOURCE] * adapters + plan[SOURCE_SLOT]]
        copies = serve(
            shrink[...], weights, scale, held, adapters * ROW_BLOCK, out, sems
        )
        for copy in copies:
            copy.wait()

    @pl.when(jnp.logical_not(visited))
    def _():
        held[...] = jnp.zeros_like(held)
        copy = pltpu.make_async_copy(
            held, out.at[:, pl.ds(adapters * ROW_BLOCK, ROW_BLOCK), :], sems.at[0]
        )
        copy.start()
        copy.wait()


def paired(replicas, hidden, down_weight, up_weight, scales, gain, lengths, moves):
    adapters, rank, width = down_weight.shape
    steps = hidden.shape[0]
    rows = steps * ROW_BLOCK
    shape = jax.ShapeDtypeStruct

    plan, block = pl.pallas_call(
        cut_kernel,
        out_shape=[shape((4,), jnp.int32), shape((rank, width), BF16)],
        in_specs=[SMEM, ANY],
        out_specs=[SMEM, ANY],
        scratch_shapes=[pltpu.SemaphoreType.DMA],
        compiler_params=params(),
        cost_estimate=pl.CostEstimate(
            flops=0, bytes_accessed=4 * rank * width, transcendentals=0
        ),
        name="cut",
    )(moves, up_weight)

    def swap(bits):
        partners = [(i, i ^ bits) for i in range(replicas)]

        def branch(block, plan, hidden, down_weight, up_weight, scales, gain, lengths):
            visiting = lax.ppermute(block, "replica", partners)
            mine = pl.pallas_call(
                project_kernel,
                out_shape=shape((adapters, rows, 2 * rank), F32),
                in_specs=[VMEM] * 3,
                out_specs=VMEM,
                compiler_params=params(),
                cost_estimate=pl.CostEstimate(
                    flops=4 * adapters * rows * rank * width,
                    bytes_accessed=4 * adapters * rows * width,
                    transcendentals=0,
                ),
                name="project",
            )(hidden, down_weight, gain)
            other = lax.ppermute(mine, "tensor", [(0, 1), (1, 0)])
            kept, leaving = pl.pallas_call(
                shrink_kernel,
                out_shape=[shape((adapters, rows, rank), BF16), shape((rows, rank), BF16)],
                in_specs=[SMEM, SMEM, VMEM, VMEM],
                out_specs=[VMEM, VMEM],
                compiler_params=params(),
                name="shrink",
            )(plan, lengths, mine, other)
            arriving = lax.ppermute(leaving, "replica", partners)
            out = pl.pallas_call(
                resident_kernel,
                out_shape=shape((steps, (adapters + 1) * ROW_BLOCK, width), BF16),
                in_specs=[SMEM, VMEM, VMEM],
                out_specs=ANY,
                scratch_shapes=[
                    pltpu.VMEM((adapters, steps, ROW_BLOCK, width), BF16),
                    pltpu.SemaphoreType.DMA((adapters, width // 1024)),
                ],
                compiler_params=params(),
                cost_estimate=pl.CostEstimate(
                    flops=2 * adapters * rows * rank * width,
                    bytes_accessed=4 * adapters * rows * width,
                    transcendentals=0,
                ),
                name="resident",
            )(scales, kept, up_weight)
            return visiting, arriving, out

        return branch

    visiting, arriving, out = lax.switch(
        plan[PARTNER] - 1,
        [swap(bits) for bits in range(1, replicas)],
        block,
        plan,
        hidden,
        down_weight,
        up_weight,
        scales,
        gain.reshape(1, width),
        lengths,
    )
    return pl.pallas_call(
        guest_kernel,
        out_shape=shape(out.shape, BF16),
        in_specs=[SMEM, SMEM, VMEM, VMEM, ANY],
        out_specs=ANY,
        scratch_shapes=[
            pltpu.VMEM((steps, ROW_BLOCK, width), BF16),
            pltpu.SemaphoreType.DMA((width // 1024,)),
        ],
        input_output_aliases={4: 0},
        compiler_params=params(),
        cost_estimate=pl.CostEstimate(
            flops=2 * rows * rank * width,
            bytes_accessed=2 * (rank + rows) * width,
            transcendentals=0,
        ),
        name="guest",
    )(plan, scales, visiting, arriving, out)


def summed(hidden, down_weight, up_weight, scales, gain, lengths, moves):
    adapters, rank, width = down_weight.shape
    steps = hidden.shape[0]
    segment = hidden.shape[1] // adapters
    me = lax.axis_index("replica")
    first = me * adapters
    sources, slots, targets = moves[:, 0], moves[:, 1], moves[:, 2]
    here = lax.dynamic_slice_in_dim(lengths, first, adapters)
    alive = jnp.arange(segment, dtype=jnp.int32)[None, :] < here[:, None]
    values = jnp.where(
        alive[None, :, :, None], hidden.reshape(steps, adapters, segment, width), 0
    ).astype(F32)
    squares = lax.psum(jnp.sum(values * values, axis=3), "tensor")
    normed = (values * lax.rsqrt(squares[..., None] / MODEL_WIDTH + EPSILON) * gain).astype(BF16)
    shrink = jnp.einsum("tnsd,nrd->tnsr", normed, down_weight, preferred_element_type=F32)
    shrink = lax.psum(shrink, "tensor").astype(BF16)
    delta = jnp.einsum("tnsr,nrd->tnsd", shrink, up_weight, preferred_element_type=F32)
    scale = lax.dynamic_slice_in_dim(scales, first, adapters)
    served = (delta * scale[None, :, None, None]).astype(BF16)
    leaving = sources == me
    slot = jnp.sum(jnp.where(leaving, slots, 0))
    parcel = lax.dynamic_index_in_dim(served, slot, 1, keepdims=False)
    guest = jnp.zeros_like(parcel)
    for move in range(MOVES):
        arrived = lax.psum(jnp.where(leaving[move], parcel, jnp.zeros_like(parcel)), "replica")
        guest = jnp.where(targets[move] == me, arrived, guest)
    removed = (jnp.arange(adapters) == slot) & jnp.any(leaving)
    served = jnp.where(removed[None, :, None, None], jnp.zeros_like(served), served)
    result = jnp.concatenate([served, guest[:, None]], axis=1)
    return result.reshape(steps, (adapters + 1) * segment, width)


def solution(mesh):
    replicas = mesh.shape["replica"]
    body = functools.partial(paired, replicas) if replicas == 2 * MOVES else summed
    return jax.shard_map(
        body,
        mesh=mesh,
        in_specs=(
            P(None, ("groups", "replica"), "tensor"),
            P("replica", None, "tensor"),
            P("replica", None, "tensor"),
            P(),
            P("tensor"),
            P("groups"),
            P("groups", None),
        ),
        out_specs=P(None, ("groups", "replica"), "tensor"),
        check_vma=False,
    )
```

```python
import functools

import jax
import jax.numpy as jnp
from jax import lax
from jax.experimental import pallas as pl
from jax.experimental.pallas import tpu as pltpu
from jax.sharding import PartitionSpec as P

MODEL_WIDTH = 8192
MOVES = 4
EPSILON = 1e-05
ROW_BLOCK = 16
VMEM_LIMIT = 48 * 1024 * 1024

SMEM = pl.BlockSpec(memory_space=pltpu.SMEM)
VMEM = pl.BlockSpec(memory_space=pltpu.VMEM)
ANY = pl.BlockSpec(memory_space=pl.ANY)
HBM = pl.BlockSpec(memory_space=pltpu.HBM)
F32 = jnp.float32
BF16 = jnp.bfloat16


def params():
    return pltpu.CompilerParams(vmem_limit_bytes=VMEM_LIMIT)


def scalar_rows(moves, column, value, pick, otherwise):
    found = otherwise
    for move in range(MOVES):
        found = jnp.where(moves[move, column] == value, moves[move, pick], found)
    return found


BRANCH, LEAVING, SOURCE, SOURCE_SLOT = range(4)
CHUNK = 1024
HALVES = 1


def cut_kernel(moves_in, up, plan_out, *refs):
    outs, (moves, plan, moves_sem, plan_sem, sems) = refs[:HALVES], refs[HALVES:]
    fetch = pltpu.make_async_copy(moves_in, moves, moves_sem)
    fetch.start()
    me = lax.axis_index("replica")
    fetch.wait()
    nothing = jnp.int32(-1)
    leaving = scalar_rows(moves, 0, me, 1, nothing)
    slot = jnp.maximum(leaving, 0)
    part = up.shape[2] // HALVES
    copies = [
        pltpu.make_async_copy(
            up.at[slot, pl.ds(row, ROW_BLOCK), pl.ds(h * part, part)],
            out.at[pl.ds(row, ROW_BLOCK)],
            sems.at[h, row // ROW_BLOCK],
        )
        for h, out in enumerate(outs)
        for row in range(0, up.shape[1], ROW_BLOCK)
    ]
    for copy in copies:
        copy.start()
    source = scalar_rows(moves, 2, me, 0, nothing)
    target = scalar_rows(moves, 0, me, 2, nothing)
    start = jnp.where(leaving >= 0, me, source)
    end = jnp.where(leaving >= 0, target, me)
    plan[BRANCH] = (start ^ end) - 1
    plan[LEAVING] = leaving
    plan[SOURCE] = source
    plan[SOURCE_SLOT] = scalar_rows(moves, 2, me, 1, nothing)
    tell = pltpu.make_async_copy(plan, plan_out, plan_sem)
    tell.start()
    for copy in copies:
        copy.wait()
    tell.wait()


def project_kernel(hidden, down, gain, out):
    adapters, rank, width = down.shape
    steps = hidden.shape[0]
    chunk = 512
    for n in range(adapters):
        total = jnp.zeros((steps * ROW_BLOCK, rank), F32)
        squares = jnp.zeros((steps * ROW_BLOCK, 1), F32)
        for c in range(0, width, chunk):
            values = hidden[:, n * ROW_BLOCK : (n + 1) * ROW_BLOCK, c : c + chunk]
            values = values.reshape(steps * ROW_BLOCK, chunk).astype(F32)
            squares += jnp.sum(values * values, axis=1, keepdims=True)
            gained = values * gain[:, c : c + chunk]
            high = gained.astype(BF16)
            low = (gained - high.astype(F32)).astype(BF16)
            weights = down[n, :, c : c + chunk]
            for part in (high, low):
                total += lax.dot_general(
                    part, weights, (((1,), (1,)), ((), ())), preferred_element_type=F32
                )
        out[n] = jnp.concatenate(
            [total, jnp.broadcast_to(squares, (steps * ROW_BLOCK, rank))], axis=1
        )


def shrink_kernel(plan, lengths, scales, mine, other, kept, leaving_out, guest_scale):
    first = lax.axis_index("replica") * mine.shape[0]
    adapters, rows, lanes = mine.shape
    rank = lanes // 2
    leaving = jnp.zeros((rows, rank), F32)
    for n in range(adapters):
        total = mine[n] + other[n]
        squares = total[:, rank : rank + 1]
        shrink = total[:, :rank] * lax.rsqrt(squares / MODEL_WIDTH + EPSILON)
        place = lax.broadcasted_iota(jnp.int32, (rows, rank), 0) % ROW_BLOCK
        shrink = jnp.where(place < lengths[first + n], shrink, 0.0)
        removed = plan[LEAVING] == n
        leaving = jnp.where(removed, shrink, leaving)
        kept[n] = jnp.where(removed, 0.0, shrink).astype(BF16)
    leaving_out[...] = leaving.astype(BF16)
    guest = jnp.maximum(plan[SOURCE], 0) * adapters + jnp.maximum(plan[SOURCE_SLOT], 0)
    guest_scale[...] = jnp.full(guest_scale.shape, scales[guest], F32)


def serve(shrink, weights, scale, held, row, first, out, sems):
    steps = held.shape[0]
    copies = []
    for k, c in enumerate(range(0, weights.shape[-1], CHUNK)):
        delta = jnp.dot(shrink, weights[:, c : c + CHUNK], preferred_element_type=F32)
        held[:, :, c : c + CHUNK] = (
            (delta * scale).astype(BF16).reshape(steps, ROW_BLOCK, CHUNK)
        )
        copy = pltpu.make_async_copy(
            held.at[:, :, c : c + CHUNK],
            out.at[:, pl.ds(row, ROW_BLOCK), pl.ds(first + c, CHUNK)],
            sems.at[k],
        )
        copy.start()
        copies.append(copy)
    return copies


def resident_kernel(scales, kept, up, out, held, sems):
    first = lax.axis_index("replica") * up.shape[0]
    copies = []
    for n in range(up.shape[0]):
        copies += serve(
            kept[n], up.at[n], scales[first + n], held.at[n], n * ROW_BLOCK, 0, out, sems.at[n]
        )
    for copy in copies:
        copy.wait()


def guest_kernel(half, scale, block, shrink, _, out, held, sems):
    row, width = out.shape[1] - ROW_BLOCK, block.shape[1]
    copies = serve(shrink[...], block, scale[0, 0], held, row, half * width, out, sems)
    for copy in copies:
        copy.wait()


def paired(replicas, hidden, down_weight, up_weight, scales, gain, lengths, moves):
    adapters, rank, width = down_weight.shape
    steps = hidden.shape[0]
    rows = steps * ROW_BLOCK
    shape = jax.ShapeDtypeStruct

    part = width // HALVES
    plan, *blocks = pl.pallas_call(
        cut_kernel,
        out_shape=[shape((4,), jnp.int32)] + [shape((rank, part), BF16)] * HALVES,
        in_specs=[HBM, HBM],
        out_specs=[ANY] + [ANY] * HALVES,
        scratch_shapes=[
            pltpu.SMEM(moves.shape, jnp.int32),
            pltpu.SMEM((4,), jnp.int32),
            pltpu.SemaphoreType.DMA,
            pltpu.SemaphoreType.DMA,
            pltpu.SemaphoreType.DMA((HALVES, rank // ROW_BLOCK)),
        ],
        compiler_params=params(),
        cost_estimate=pl.CostEstimate(
            flops=0, bytes_accessed=4 * rank * width, transcendentals=0
        ),
        name="cut",
    )(moves, up_weight)

    def swap(bits):
        partners = [(i, i ^ bits) for i in range(replicas)]

        def branch(blocks, plan, hidden, down_weight, up_weight, scales, gain, lengths):
            visiting = [lax.ppermute(block, "replica", partners) for block in blocks]
            mine = pl.pallas_call(
                project_kernel,
                out_shape=shape((adapters, rows, 2 * rank), F32),
                in_specs=[VMEM] * 3,
                out_specs=VMEM,
                compiler_params=params(),
                cost_estimate=pl.CostEstimate(
                    flops=4 * adapters * rows * rank * width,
                    bytes_accessed=4 * adapters * rows * width,
                    transcendentals=0,
                ),
                name="project",
            )(hidden, down_weight, gain)
            other = lax.ppermute(mine, "tensor", [(0, 1), (1, 0)])
            kept, leaving, guest_scale = pl.pallas_call(
                shrink_kernel,
                out_shape=[
                    shape((adapters, rows, rank), BF16),
                    shape((rows, rank), BF16),
                    shape((8, 128), F32),
                ],
                in_specs=[SMEM, SMEM, SMEM, VMEM, VMEM],
                out_specs=[VMEM] * 3,
                compiler_params=params(),
                name="shrink",
            )(plan, lengths, scales, mine, other)
            arriving = lax.ppermute(leaving, "replica", partners)
            out_shape = shape((steps, (adapters + 1) * ROW_BLOCK, width), BF16)
            out = pl.pallas_call(
                resident_kernel,
                out_shape=out_shape,
                in_specs=[SMEM, VMEM, VMEM],
                out_specs=HBM,
                scratch_shapes=[
                    pltpu.VMEM((adapters, steps, ROW_BLOCK, width), BF16),
                    pltpu.SemaphoreType.DMA((adapters, width // CHUNK)),
                ],
                compiler_params=params(),
                cost_estimate=pl.CostEstimate(
                    flops=2 * adapters * rows * rank * width,
                    bytes_accessed=4 * adapters * rows * width,
                    transcendentals=0,
                ),
                name="resident",
            )(scales, kept, up_weight)
            for half, block in enumerate(visiting):
                out = pl.pallas_call(
                    functools.partial(guest_kernel, half),
                    out_shape=out_shape,
                    in_specs=[VMEM, VMEM, VMEM, HBM],
                    out_specs=HBM,
                    scratch_shapes=[
                        pltpu.VMEM((steps, ROW_BLOCK, part), BF16),
                        pltpu.SemaphoreType.DMA((part // CHUNK,)),
                    ],
                    input_output_aliases={3: 0},
                    compiler_params=params(),
                    cost_estimate=pl.CostEstimate(
                        flops=2 * rows * rank * part,
                        bytes_accessed=2 * (rank + rows) * part,
                        transcendentals=0,
                    ),
                    name="guest",
                )(guest_scale, block, arriving, out)
            return out

        return branch

    return lax.switch(
        plan[BRANCH],
        [swap(bits) for bits in range(1, replicas)],
        blocks,
        plan,
        hidden,
        down_weight,
        up_weight,
        scales,
        gain.reshape(1, width),
        lengths,
    )


def summed(hidden, down_weight, up_weight, scales, gain, lengths, moves):
    adapters, rank, width = down_weight.shape
    steps = hidden.shape[0]
    segment = hidden.shape[1] // adapters
    me = lax.axis_index("replica")
    first = me * adapters
    sources, slots, targets = moves[:, 0], moves[:, 1], moves[:, 2]
    here = lax.dynamic_slice_in_dim(lengths, first, adapters)
    alive = jnp.arange(segment, dtype=jnp.int32)[None, :] < here[:, None]
    values = jnp.where(
        alive[None, :, :, None], hidden.reshape(steps, adapters, segment, width), 0
    ).astype(F32)
    squares = lax.psum(jnp.sum(values * values, axis=3), "tensor")
    normed = (values * lax.rsqrt(squares[..., None] / MODEL_WIDTH + EPSILON) * gain).astype(BF16)
    shrink = jnp.einsum("tnsd,nrd->tnsr", normed, down_weight, preferred_element_type=F32)
    shrink = lax.psum(shrink, "tensor").astype(BF16)
    delta = jnp.einsum("tnsr,nrd->tnsd", shrink, up_weight, preferred_element_type=F32)
    scale = lax.dynamic_slice_in_dim(scales, first, adapters)
    served = (delta * scale[None, :, None, None]).astype(BF16)
    leaving = sources == me
    slot = jnp.sum(jnp.where(leaving, slots, 0))
    parcel = lax.dynamic_index_in_dim(served, slot, 1, keepdims=False)
    guest = jnp.zeros_like(parcel)
    for move in range(MOVES):
        arrived = lax.psum(jnp.where(leaving[move], parcel, jnp.zeros_like(parcel)), "replica")
        guest = jnp.where(targets[move] == me, arrived, guest)
    removed = (jnp.arange(adapters) == slot) & jnp.any(leaving)
    served = jnp.where(removed[None, :, None, None], jnp.zeros_like(served), served)
    result = jnp.concatenate([served, guest[:, None]], axis=1)
    return result.reshape(steps, (adapters + 1) * segment, width)


def solution(mesh):
    replicas = mesh.shape["replica"]
    body = functools.partial(paired, replicas) if replicas == 2 * MOVES else summed
    return jax.shard_map(
        body,
        mesh=mesh,
        in_specs=(
            P(None, ("groups", "replica"), "tensor"),
            P("replica", None, "tensor"),
            P("replica", None, "tensor"),
            P(),
            P("tensor"),
            P("groups"),
            P("groups", None),
        ),
        out_specs=P(None, ("groups", "replica"), "tensor"),
        check_vma=False,
    )
```

```python
import functools

import jax
import jax.numpy as jnp
from jax import lax
from jax.experimental import pallas as pl
from jax.experimental.pallas import tpu as pltpu
from jax.sharding import PartitionSpec as P

MODEL_WIDTH = 8192
MOVES = 4
COLUMNS = 2
EPSILON = 1e-05
ROW_BLOCK = 16
VMEM_LIMIT = 48 * 1024 * 1024

SMEM = pl.BlockSpec(memory_space=pltpu.SMEM)
VMEM = pl.BlockSpec(memory_space=pltpu.VMEM)
ANY = pl.BlockSpec(memory_space=pl.ANY)
HBM = pl.BlockSpec(memory_space=pltpu.HBM)
F32 = jnp.float32
BF16 = jnp.bfloat16


def params():
    return pltpu.CompilerParams(vmem_limit_bytes=VMEM_LIMIT)


def scalar_rows(moves, column, value, pick, otherwise):
    found = otherwise
    for move in range(MOVES):
        found = jnp.where(moves[move, column] == value, moves[move, pick], found)
    return found


BRANCH, LEAVING, SOURCE, SOURCE_SLOT = range(4)
CHUNK = 1024


def crowded(moves, both_ways):
    def sent(start, end):
        low = jnp.minimum(start // COLUMNS, end // COLUMNS)
        high = jnp.maximum(start // COLUMNS, end // COLUMNS)
        links = ((1 << (8 * high)) - (1 << (8 * low))) & 0x010101
        links = links << (4 * (start % COLUMNS))
        up = start < end
        return jnp.where(up, links, 0), jnp.where(up, 0, links)

    up, down = jnp.int32(0), jnp.int32(0)
    for move in range(MOVES):
        source, target = moves[move, 0], moves[move, 2]
        for start, end in ((source, target), (target, source))[: 1 + both_ways]:
            more_up, more_down = sent(start, end)
            up, down = up + more_up, down + more_down
    return ((up | down) & 0xEEEEEE) != 0


def cut_kernel(replicas, moves_in, up, plan_out, out, moves, plan, moves_sem, plan_sem, sems):
    fetch = pltpu.make_async_copy(moves_in, moves, moves_sem)
    fetch.start()
    me = lax.axis_index("replica")
    fetch.wait()
    nothing = jnp.int32(-1)
    leaving = scalar_rows(moves, 0, me, 1, nothing)
    slot = jnp.maximum(leaving, 0)
    copies = [
        pltpu.make_async_copy(
            up.at[slot, pl.ds(row, ROW_BLOCK)],
            out.at[pl.ds(row, ROW_BLOCK)],
            sems.at[row // ROW_BLOCK],
        )
        for row in range(0, up.shape[1], ROW_BLOCK)
    ]
    for copy in copies:
        copy.start()
    source = scalar_rows(moves, 2, me, 0, nothing)
    target = scalar_rows(moves, 0, me, 2, nothing)
    start = jnp.where(leaving >= 0, me, source)
    end = jnp.where(leaving >= 0, target, me)
    bits = (start ^ end) - 1
    one_way = jnp.logical_and(crowded(moves, True), jnp.logical_not(crowded(moves, False)))
    plan[BRANCH] = jnp.where(one_way, replicas - 1 + 2 * bits + jnp.where(start < end, 0, 1), bits)
    plan[LEAVING] = leaving
    plan[SOURCE] = source
    plan[SOURCE_SLOT] = scalar_rows(moves, 2, me, 1, nothing)
    tell = pltpu.make_async_copy(plan, plan_out, plan_sem)
    tell.start()
    for copy in copies:
        copy.wait()
    tell.wait()


def project_kernel(hidden, down, gain, out):
    adapters, rank, width = down.shape
    steps = hidden.shape[0]
    rows, chunk, lanes = steps * ROW_BLOCK, 512, 128

    @pl.loop(0, adapters)
    def _(n):
        place = pl.ds(pl.multiple_of(n * ROW_BLOCK, ROW_BLOCK), ROW_BLOCK)

        def add(c, sums):
            total, squares = sums
            columns = pl.ds(pl.multiple_of(c * chunk, chunk), chunk)
            values = hidden[:, place, columns].reshape(rows, chunk).astype(F32)
            for k in range(0, chunk, lanes):
                squares += values[:, k : k + lanes] * values[:, k : k + lanes]
            gained = values * gain[:, columns]
            high = gained.astype(BF16)
            low = (gained - high.astype(F32)).astype(BF16)
            weights = down[n, :, columns]
            for part in (high, low):
                total += lax.dot_general(
                    part, weights, (((1,), (1,)), ((), ())), preferred_element_type=F32
                )
            return total, squares

        total, squares = lax.fori_loop(
            0, width // chunk, add, (jnp.zeros((rows, rank), F32), jnp.zeros((rows, lanes), F32))
        )
        squares = jnp.sum(squares, axis=1, keepdims=True)
        out[n] = jnp.concatenate([total, jnp.broadcast_to(squares, (rows, rank))], axis=1)


def shrink_kernel(plan, lengths, scales, mine, other, kept, leaving_out, guest_scale):
    first = lax.axis_index("replica") * mine.shape[0]
    adapters, rows, lanes = mine.shape
    rank = lanes // 2
    leaving = jnp.zeros((rows, rank), F32)
    for n in range(adapters):
        total = mine[n] + other[n]
        squares = total[:, rank : rank + 1]
        shrink = total[:, :rank] * lax.rsqrt(squares / MODEL_WIDTH + EPSILON)
        place = lax.broadcasted_iota(jnp.int32, (rows, rank), 0) % ROW_BLOCK
        shrink = jnp.where(place < lengths[first + n], shrink, 0.0)
        removed = plan[LEAVING] == n
        leaving = jnp.where(removed, shrink, leaving)
        kept[n] = jnp.where(removed, 0.0, shrink).astype(BF16)
    leaving_out[...] = leaving.astype(BF16)
    guest = jnp.maximum(plan[SOURCE], 0) * adapters + jnp.maximum(plan[SOURCE_SLOT], 0)
    guest_scale[...] = jnp.full(guest_scale.shape, scales[guest], F32)


def serve(shrink, weights, scale, held, row, out, sems):
    steps = held.shape[0]

    @pl.loop(0, weights.shape[-1] // CHUNK)
    def _(k):
        columns = pl.ds(pl.multiple_of(k * CHUNK, CHUNK), CHUNK)
        delta = jnp.dot(shrink, weights[:, columns], preferred_element_type=F32)
        held[:, :, columns] = (delta * scale).astype(BF16).reshape(steps, ROW_BLOCK, CHUNK)
        served_copy(k, held, row, out, sems).start()


def served_copy(k, held, row, out, sems):
    columns = pl.ds(pl.multiple_of(k * CHUNK, CHUNK), CHUNK)
    rows = pl.ds(pl.multiple_of(row, ROW_BLOCK), ROW_BLOCK)
    return pltpu.make_async_copy(held.at[:, :, columns], out.at[:, rows, columns], sems.at[k])


def resident_kernel(scales, kept, up, out, held, sems):
    first = lax.axis_index("replica") * up.shape[0]

    @pl.loop(0, up.shape[0])
    def _(n):
        serve(kept[n], up.at[n], scales[first + n], held.at[n], n * ROW_BLOCK, out, sems.at[n])

    @pl.loop(0, up.shape[0])
    def _(n):
        @pl.loop(0, up.shape[2] // CHUNK)
        def _(k):
            served_copy(k, held.at[n], n * ROW_BLOCK, out, sems.at[n]).wait()


def guest_kernel(scale, block, shrink, _, out, held, sems):
    row = out.shape[1] - ROW_BLOCK
    serve(shrink[...], block, scale[0, 0], held, row, out, sems)

    @pl.loop(0, block.shape[1] // CHUNK)
    def _(k):
        served_copy(k, held, row, out, sems).wait()


def paired(replicas, hidden, down_weight, up_weight, scales, gain, lengths, moves):
    adapters, rank, width = down_weight.shape
    steps = hidden.shape[0]
    rows = steps * ROW_BLOCK
    shape = jax.ShapeDtypeStruct

    plan, block = pl.pallas_call(
        functools.partial(cut_kernel, replicas),
        out_shape=[shape((4,), jnp.int32), shape((rank, width), BF16)],
        in_specs=[HBM, HBM],
        out_specs=[ANY, ANY],
        scratch_shapes=[
            pltpu.SMEM(moves.shape, jnp.int32),
            pltpu.SMEM((4,), jnp.int32),
            pltpu.SemaphoreType.DMA,
            pltpu.SemaphoreType.DMA,
            pltpu.SemaphoreType.DMA((rank // ROW_BLOCK,)),
        ],
        compiler_params=params(),
        cost_estimate=pl.CostEstimate(
            flops=0, bytes_accessed=4 * rank * width, transcendentals=0
        ),
        name="cut",
    )(moves, up_weight)

    def swap(bits, *upward):
        partners = [(i, i ^ bits) for i in range(replicas)]
        across = [(i, k) for i, k in partners if not upward or (i < k) == upward[0]]

        def branch(block, plan, hidden, down_weight, up_weight, scales, gain, lengths):
            visiting = lax.ppermute(block, "replica", across)
            mine = pl.pallas_call(
                project_kernel,
                out_shape=shape((adapters, rows, 2 * rank), F32),
                in_specs=[VMEM] * 3,
                out_specs=VMEM,
                compiler_params=params(),
                cost_estimate=pl.CostEstimate(
                    flops=4 * adapters * rows * rank * width,
                    bytes_accessed=4 * adapters * rows * width,
                    transcendentals=0,
                ),
                name="project",
            )(hidden, down_weight, gain)
            other = lax.ppermute(mine, "tensor", [(0, 1), (1, 0)])
            kept, leaving, guest_scale = pl.pallas_call(
                shrink_kernel,
                out_shape=[
                    shape((adapters, rows, rank), BF16),
                    shape((rows, rank), BF16),
                    shape((8, 128), F32),
                ],
                in_specs=[SMEM, SMEM, SMEM, VMEM, VMEM],
                out_specs=[VMEM] * 3,
                compiler_params=params(),
                name="shrink",
            )(plan, lengths, scales, mine, other)
            arriving = lax.ppermute(leaving, "replica", partners)
            out_shape = shape((steps, (adapters + 1) * ROW_BLOCK, width), BF16)
            out = pl.pallas_call(
                resident_kernel,
                out_shape=out_shape,
                in_specs=[SMEM, VMEM, VMEM],
                out_specs=HBM,
                scratch_shapes=[
                    pltpu.VMEM((adapters, steps, ROW_BLOCK, width), BF16),
                    pltpu.SemaphoreType.DMA((adapters, width // CHUNK)),
                ],
                compiler_params=params(),
                cost_estimate=pl.CostEstimate(
                    flops=2 * adapters * rows * rank * width,
                    bytes_accessed=4 * adapters * rows * width,
                    transcendentals=0,
                ),
                name="resident",
            )(scales, kept, up_weight)
            return pl.pallas_call(
                guest_kernel,
                out_shape=out_shape,
                in_specs=[VMEM, VMEM, VMEM, HBM],
                out_specs=HBM,
                scratch_shapes=[
                    pltpu.VMEM((steps, ROW_BLOCK, width), BF16),
                    pltpu.SemaphoreType.DMA((width // CHUNK,)),
                ],
                input_output_aliases={3: 0},
                compiler_params=params(),
                cost_estimate=pl.CostEstimate(
                    flops=2 * rows * rank * width,
                    bytes_accessed=2 * (rank + rows) * width,
                    transcendentals=0,
                ),
                name="guest",
            )(guest_scale, visiting, arriving, out)

        return branch

    return lax.switch(
        plan[BRANCH],
        [swap(bits) for bits in range(1, replicas)]
        + [swap(bits, upward) for bits in range(1, replicas) for upward in (True, False)],
        block,
        plan,
        hidden,
        down_weight,
        up_weight,
        scales,
        gain.reshape(1, width),
        lengths,
    )


def summed(hidden, down_weight, up_weight, scales, gain, lengths, moves):
    adapters, rank, width = down_weight.shape
    steps = hidden.shape[0]
    segment = hidden.shape[1] // adapters
    me = lax.axis_index("replica")
    first = me * adapters
    sources, slots, targets = moves[:, 0], moves[:, 1], moves[:, 2]
    here = lax.dynamic_slice_in_dim(lengths, first, adapters)
    alive = jnp.arange(segment, dtype=jnp.int32)[None, :] < here[:, None]
    values = jnp.where(
        alive[None, :, :, None], hidden.reshape(steps, adapters, segment, width), 0
    ).astype(F32)
    squares = lax.psum(jnp.sum(values * values, axis=3), "tensor")
    normed = (values * lax.rsqrt(squares[..., None] / MODEL_WIDTH + EPSILON) * gain).astype(BF16)
    shrink = jnp.einsum("tnsd,nrd->tnsr", normed, down_weight, preferred_element_type=F32)
    shrink = lax.psum(shrink, "tensor").astype(BF16)
    delta = jnp.einsum("tnsr,nrd->tnsd", shrink, up_weight, preferred_element_type=F32)
    scale = lax.dynamic_slice_in_dim(scales, first, adapters)
    served = (delta * scale[None, :, None, None]).astype(BF16)
    leaving = sources == me
    slot = jnp.sum(jnp.where(leaving, slots, 0))
    parcel = lax.dynamic_index_in_dim(served, slot, 1, keepdims=False)
    guest = jnp.zeros_like(parcel)
    for move in range(MOVES):
        arrived = lax.psum(jnp.where(leaving[move], parcel, jnp.zeros_like(parcel)), "replica")
        guest = jnp.where(targets[move] == me, arrived, guest)
    removed = (jnp.arange(adapters) == slot) & jnp.any(leaving)
    served = jnp.where(removed[None, :, None, None], jnp.zeros_like(served), served)
    result = jnp.concatenate([served, guest[:, None]], axis=1)
    return result.reshape(steps, (adapters + 1) * segment, width)


def solution(mesh):
    replicas = mesh.shape["replica"]
    body = functools.partial(paired, replicas) if replicas == 2 * MOVES else summed
    return jax.shard_map(
        body,
        mesh=mesh,
        in_specs=(
            P(None, ("groups", "replica"), "tensor"),
            P("replica", None, "tensor"),
            P("replica", None, "tensor"),
            P(),
            P("tensor"),
            P("groups"),
            P("groups", None),
        ),
        out_specs=P(None, ("groups", "replica"), "tensor"),
        check_vma=False,
    )
```

```python
import functools

import jax
import jax.numpy as jnp
from jax import lax
from jax.experimental import pallas as pl
from jax.experimental.pallas import tpu as pltpu
from jax.sharding import PartitionSpec as P

MODEL_WIDTH = 8192
MOVES = 4
COLUMNS = 2
EPSILON = 1e-05
ROW_BLOCK = 16
VMEM_LIMIT = 48 * 1024 * 1024

SMEM = pl.BlockSpec(memory_space=pltpu.SMEM)
VMEM = pl.BlockSpec(memory_space=pltpu.VMEM)
ANY = pl.BlockSpec(memory_space=pl.ANY)
HBM = pl.BlockSpec(memory_space=pltpu.HBM)
F32 = jnp.float32
BF16 = jnp.bfloat16


def params():
    return pltpu.CompilerParams(vmem_limit_bytes=VMEM_LIMIT)


def scalar_rows(moves, column, value, pick, otherwise):
    found = otherwise
    for move in range(MOVES):
        found = jnp.where(moves[move, column] == value, moves[move, pick], found)
    return found


BRANCH, LEAVING, SOURCE, SOURCE_SLOT = range(4)
CHUNK = 1024


def crowded(moves, both_ways):
    def sent(start, end):
        low = jnp.minimum(start // COLUMNS, end // COLUMNS)
        high = jnp.maximum(start // COLUMNS, end // COLUMNS)
        links = ((1 << (8 * high)) - (1 << (8 * low))) & 0x010101
        links = links << (4 * (start % COLUMNS))
        up = start < end
        return jnp.where(up, links, 0), jnp.where(up, 0, links)

    up, down = jnp.int32(0), jnp.int32(0)
    for move in range(MOVES):
        source, target = moves[move, 0], moves[move, 2]
        for start, end in ((source, target), (target, source))[: 1 + both_ways]:
            more_up, more_down = sent(start, end)
            up, down = up + more_up, down + more_down
    return ((up | down) & 0xEEEEEE) != 0


def cut_kernel(replicas, moves_in, up, plan, out, moves, moves_sem, sems):
    fetch = pltpu.make_async_copy(moves_in, moves, moves_sem)
    fetch.start()
    me = lax.axis_index("replica")
    fetch.wait()
    nothing = jnp.int32(-1)
    leaving = scalar_rows(moves, 0, me, 1, nothing)
    slot = jnp.maximum(leaving, 0)
    copies = [
        pltpu.make_async_copy(
            up.at[slot, pl.ds(row, ROW_BLOCK)],
            out.at[pl.ds(row, ROW_BLOCK)],
            sems.at[row // ROW_BLOCK],
        )
        for row in range(0, up.shape[1], ROW_BLOCK)
    ]
    for copy in copies:
        copy.start()
    source = scalar_rows(moves, 2, me, 0, nothing)
    target = scalar_rows(moves, 0, me, 2, nothing)
    start = jnp.where(leaving >= 0, me, source)
    end = jnp.where(leaving >= 0, target, me)
    bits = (start ^ end) - 1
    one_way = jnp.logical_and(crowded(moves, True), jnp.logical_not(crowded(moves, False)))
    plan[BRANCH] = jnp.where(one_way, replicas - 1 + 2 * bits + jnp.where(start < end, 0, 1), bits)
    plan[LEAVING] = leaving
    plan[SOURCE] = source
    plan[SOURCE_SLOT] = scalar_rows(moves, 2, me, 1, nothing)
    for copy in copies:
        copy.wait()


def project_kernel(hidden, down, gain, out):
    adapters, rank, width = down.shape
    steps = hidden.shape[0]
    rows, chunk, lanes = steps * ROW_BLOCK, 512, 128

    @pl.loop(0, adapters)
    def _(n):
        place = pl.ds(pl.multiple_of(n * ROW_BLOCK, ROW_BLOCK), ROW_BLOCK)

        def add(c, sums):
            total, squares = sums
            columns = pl.ds(pl.multiple_of(c * chunk, chunk), chunk)
            values = hidden[:, place, columns].reshape(rows, chunk).astype(F32)
            for k in range(0, chunk, lanes):
                squares += values[:, k : k + lanes] * values[:, k : k + lanes]
            gained = values * gain[:, columns]
            high = gained.astype(BF16)
            low = (gained - high.astype(F32)).astype(BF16)
            weights = down[n, :, columns]
            for part in (high, low):
                total += lax.dot_general(
                    part, weights, (((1,), (1,)), ((), ())), preferred_element_type=F32
                )
            return total, squares

        total, squares = lax.fori_loop(
            0, width // chunk, add, (jnp.zeros((rows, rank), F32), jnp.zeros((rows, lanes), F32))
        )
        squares = jnp.sum(squares, axis=1, keepdims=True)
        out[n] = jnp.concatenate([total, jnp.broadcast_to(squares, (rows, rank))], axis=1)


def shrink_kernel(plan, lengths, scales, mine, other, kept, leaving_out, guest_scale):
    first = lax.axis_index("replica") * mine.shape[0]
    adapters, rows, lanes = mine.shape
    rank = lanes // 2
    leaving = jnp.zeros((rows, rank), F32)
    for n in range(adapters):
        total = mine[n] + other[n]
        squares = total[:, rank : rank + 1]
        shrink = total[:, :rank] * lax.rsqrt(squares / MODEL_WIDTH + EPSILON)
        place = lax.broadcasted_iota(jnp.int32, (rows, rank), 0) % ROW_BLOCK
        shrink = jnp.where(place < lengths[first + n], shrink, 0.0)
        removed = plan[LEAVING] == n
        leaving = jnp.where(removed, shrink, leaving)
        kept[n] = jnp.where(removed, 0.0, shrink).astype(BF16)
    leaving_out[...] = leaving.astype(BF16)
    guest = jnp.maximum(plan[SOURCE], 0) * adapters + jnp.maximum(plan[SOURCE_SLOT], 0)
    guest_scale[...] = jnp.full(guest_scale.shape, scales[guest], F32)


def serve(shrink, weights, scale, held, row, out, sems):
    steps = held.shape[0]

    @pl.loop(0, weights.shape[-1] // CHUNK)
    def _(k):
        columns = pl.ds(pl.multiple_of(k * CHUNK, CHUNK), CHUNK)
        delta = jnp.dot(shrink, weights[:, columns], preferred_element_type=F32)
        held[:, :, columns] = (delta * scale).astype(BF16).reshape(steps, ROW_BLOCK, CHUNK)
        served_copy(k, held, row, out, sems).start()


def served_copy(k, held, row, out, sems):
    columns = pl.ds(pl.multiple_of(k * CHUNK, CHUNK), CHUNK)
    rows = pl.ds(pl.multiple_of(row, ROW_BLOCK), ROW_BLOCK)
    return pltpu.make_async_copy(held.at[:, :, columns], out.at[:, rows, columns], sems.at[k])


def resident_kernel(scales, kept, up, out, held, sems):
    first = lax.axis_index("replica") * up.shape[0]

    @pl.loop(0, up.shape[0])
    def _(n):
        serve(kept[n], up.at[n], scales[first + n], held.at[n], n * ROW_BLOCK, out, sems.at[n])

    @pl.loop(0, up.shape[0])
    def _(n):
        @pl.loop(0, up.shape[2] // CHUNK)
        def _(k):
            served_copy(k, held.at[n], n * ROW_BLOCK, out, sems.at[n]).wait()


def guest_kernel(scale, block, shrink, _, out, held, sems):
    row = out.shape[1] - ROW_BLOCK
    serve(shrink[...], block, scale[0, 0], held, row, out, sems)

    @pl.loop(0, block.shape[1] // CHUNK)
    def _(k):
        served_copy(k, held, row, out, sems).wait()


def paired(replicas, hidden, down_weight, up_weight, scales, gain, lengths, moves):
    adapters, rank, width = down_weight.shape
    steps = hidden.shape[0]
    rows = steps * ROW_BLOCK
    shape = jax.ShapeDtypeStruct

    plan, block = pl.pallas_call(
        functools.partial(cut_kernel, replicas),
        out_shape=[pltpu.SMEM((4,), jnp.int32), shape((rank, width), BF16)],
        in_specs=[HBM, HBM],
        out_specs=[SMEM, ANY],
        scratch_shapes=[
            pltpu.SMEM(moves.shape, jnp.int32),
            pltpu.SemaphoreType.DMA,
            pltpu.SemaphoreType.DMA((rank // ROW_BLOCK,)),
        ],
        compiler_params=params(),
        cost_estimate=pl.CostEstimate(
            flops=0, bytes_accessed=4 * rank * width, transcendentals=0
        ),
        name="cut",
    )(pltpu.with_memory_space_constraint(moves, pltpu.HBM), up_weight)

    def swap(bits, *upward):
        partners = [(i, i ^ bits) for i in range(replicas)]
        across = [(i, k) for i, k in partners if not upward or (i < k) == upward[0]]

        def branch(block, plan, hidden, down_weight, up_weight, scales, gain, lengths):
            visiting = lax.ppermute(block, "replica", across)
            mine = pl.pallas_call(
                project_kernel,
                out_shape=shape((adapters, rows, 2 * rank), F32),
                in_specs=[VMEM] * 3,
                out_specs=VMEM,
                compiler_params=params(),
                cost_estimate=pl.CostEstimate(
                    flops=4 * adapters * rows * rank * width,
                    bytes_accessed=4 * adapters * rows * width,
                    transcendentals=0,
                ),
                name="project",
            )(hidden, down_weight, gain)
            other = lax.ppermute(mine, "tensor", [(0, 1), (1, 0)])
            kept, leaving, guest_scale = pl.pallas_call(
                shrink_kernel,
                out_shape=[
                    shape((adapters, rows, rank), BF16),
                    shape((rows, rank), BF16),
                    shape((8, 128), F32),
                ],
                in_specs=[SMEM, SMEM, SMEM, VMEM, VMEM],
                out_specs=[VMEM] * 3,
                compiler_params=params(),
                name="shrink",
            )(plan, lengths, scales, mine, other)
            arriving = lax.ppermute(leaving, "replica", partners)
            out_shape = shape((steps, (adapters + 1) * ROW_BLOCK, width), BF16)
            out = pl.pallas_call(
                resident_kernel,
                out_shape=out_shape,
                in_specs=[SMEM, VMEM, VMEM],
                out_specs=HBM,
                scratch_shapes=[
                    pltpu.VMEM((adapters, steps, ROW_BLOCK, width), BF16),
                    pltpu.SemaphoreType.DMA((adapters, width // CHUNK)),
                ],
                compiler_params=params(),
                cost_estimate=pl.CostEstimate(
                    flops=2 * adapters * rows * rank * width,
                    bytes_accessed=4 * adapters * rows * width,
                    transcendentals=0,
                ),
                name="resident",
            )(scales, kept, up_weight)
            return pl.pallas_call(
                guest_kernel,
                out_shape=out_shape,
                in_specs=[VMEM, VMEM, VMEM, HBM],
                out_specs=HBM,
                scratch_shapes=[
                    pltpu.VMEM((steps, ROW_BLOCK, width), BF16),
                    pltpu.SemaphoreType.DMA((width // CHUNK,)),
                ],
                input_output_aliases={3: 0},
                compiler_params=params(),
                cost_estimate=pl.CostEstimate(
                    flops=2 * rows * rank * width,
                    bytes_accessed=2 * (rank + rows) * width,
                    transcendentals=0,
                ),
                name="guest",
            )(guest_scale, visiting, arriving, out)

        return branch

    return lax.switch(
        plan[BRANCH],
        [swap(bits) for bits in range(1, replicas)]
        + [swap(bits, upward) for bits in range(1, replicas) for upward in (True, False)],
        block,
        plan,
        hidden,
        down_weight,
        up_weight,
        scales,
        gain.reshape(1, width),
        lengths,
    )


def summed(hidden, down_weight, up_weight, scales, gain, lengths, moves):
    adapters, rank, width = down_weight.shape
    steps = hidden.shape[0]
    segment = hidden.shape[1] // adapters
    me = lax.axis_index("replica")
    first = me * adapters
    sources, slots, targets = moves[:, 0], moves[:, 1], moves[:, 2]
    here = lax.dynamic_slice_in_dim(lengths, first, adapters)
    alive = jnp.arange(segment, dtype=jnp.int32)[None, :] < here[:, None]
    values = jnp.where(
        alive[None, :, :, None], hidden.reshape(steps, adapters, segment, width), 0
    ).astype(F32)
    squares = lax.psum(jnp.sum(values * values, axis=3), "tensor")
    normed = (values * lax.rsqrt(squares[..., None] / MODEL_WIDTH + EPSILON) * gain).astype(BF16)
    shrink = jnp.einsum("tnsd,nrd->tnsr", normed, down_weight, preferred_element_type=F32)
    shrink = lax.psum(shrink, "tensor").astype(BF16)
    delta = jnp.einsum("tnsr,nrd->tnsd", shrink, up_weight, preferred_element_type=F32)
    scale = lax.dynamic_slice_in_dim(scales, first, adapters)
    served = (delta * scale[None, :, None, None]).astype(BF16)
    leaving = sources == me
    slot = jnp.sum(jnp.where(leaving, slots, 0))
    parcel = lax.dynamic_index_in_dim(served, slot, 1, keepdims=False)
    guest = jnp.zeros_like(parcel)
    for move in range(MOVES):
        arrived = lax.psum(jnp.where(leaving[move], parcel, jnp.zeros_like(parcel)), "replica")
        guest = jnp.where(targets[move] == me, arrived, guest)
    removed = (jnp.arange(adapters) == slot) & jnp.any(leaving)
    served = jnp.where(removed[None, :, None, None], jnp.zeros_like(served), served)
    result = jnp.concatenate([served, guest[:, None]], axis=1)
    return result.reshape(steps, (adapters + 1) * segment, width)


def solution(mesh):
    replicas = mesh.shape["replica"]
    body = functools.partial(paired, replicas) if replicas == 2 * MOVES else summed
    return jax.shard_map(
        body,
        mesh=mesh,
        in_specs=(
            P(None, ("groups", "replica"), "tensor"),
            P("replica", None, "tensor"),
            P("replica", None, "tensor"),
            P(),
            P("tensor"),
            P("groups"),
            P("groups", None),
        ),
        out_specs=P(None, ("groups", "replica"), "tensor"),
        check_vma=False,
    )
```

```python
import functools

import jax
import jax.numpy as jnp
from jax import lax
from jax.experimental import pallas as pl
from jax.experimental.pallas import tpu as pltpu
from jax.sharding import PartitionSpec as P

MODEL_WIDTH = 8192
MOVES = 4
COLUMNS = 2
EPSILON = 1e-05
ROW_BLOCK = 16
VMEM_LIMIT = 48 * 1024 * 1024

SMEM = pl.BlockSpec(memory_space=pltpu.SMEM)
VMEM = pl.BlockSpec(memory_space=pltpu.VMEM)
ANY = pl.BlockSpec(memory_space=pl.ANY)
HBM = pl.BlockSpec(memory_space=pltpu.HBM)
F32 = jnp.float32
BF16 = jnp.bfloat16


def params():
    return pltpu.CompilerParams(vmem_limit_bytes=VMEM_LIMIT)


def scalar_rows(moves, column, value, pick, otherwise):
    found = otherwise
    for move in range(MOVES):
        found = jnp.where(moves[move, column] == value, moves[move, pick], found)
    return found


BRANCH, LEAVING, SOURCE, SOURCE_SLOT = range(4)
CHUNK = 2048
PARTS = 2


def crowded(moves, both_ways):
    def sent(start, end):
        low = jnp.minimum(start // COLUMNS, end // COLUMNS)
        high = jnp.maximum(start // COLUMNS, end // COLUMNS)
        links = ((1 << (8 * high)) - (1 << (8 * low))) & 0x010101
        links = links << (4 * (start % COLUMNS))
        up = start < end
        return jnp.where(up, links, 0), jnp.where(up, 0, links)

    up, down = jnp.int32(0), jnp.int32(0)
    for move in range(MOVES):
        source, target = moves[move, 0], moves[move, 2]
        for start, end in ((source, target), (target, source))[: 1 + both_ways]:
            more_up, more_down = sent(start, end)
            up, down = up + more_up, down + more_down
    return ((up | down) & 0xEEEEEE) != 0


def cut_kernel(replicas, moves_in, up, plan, out, moves, held, moves_sem, sems):
    fetch = pltpu.make_async_copy(moves_in, moves, moves_sem)
    fetch.start()
    rows = up.shape[1] // PARTS
    copies = [
        pltpu.make_async_copy(
            up.at[n, pl.ds(k * rows, rows)], held.at[n, pl.ds(k * rows, rows)], sems.at[n, k]
        )
        for n in range(up.shape[0])
        for k in range(PARTS)
    ]
    for copy in copies:
        copy.start()
    me = lax.axis_index("replica")
    fetch.wait()
    nothing = jnp.int32(-1)
    leaving = scalar_rows(moves, 0, me, 1, nothing)
    source = scalar_rows(moves, 2, me, 0, nothing)
    target = scalar_rows(moves, 0, me, 2, nothing)
    start = jnp.where(leaving >= 0, me, source)
    end = jnp.where(leaving >= 0, target, me)
    bits = (start ^ end) - 1
    one_way = jnp.logical_and(crowded(moves, True), jnp.logical_not(crowded(moves, False)))
    plan[BRANCH] = jnp.where(one_way, replicas - 1 + 2 * bits + jnp.where(start < end, 0, 1), bits)
    plan[LEAVING] = leaving
    plan[SOURCE] = source
    plan[SOURCE_SLOT] = scalar_rows(moves, 2, me, 1, nothing)
    for copy in copies:
        copy.wait()
    out[...] = held[jnp.maximum(leaving, 0)]


def project_kernel(hidden, down, gain, out):
    adapters, rank, width = down.shape
    steps = hidden.shape[0]
    rows, chunk, lanes = steps * ROW_BLOCK, 512, 128

    @pl.loop(0, adapters)
    def _(n):
        place = pl.ds(pl.multiple_of(n * ROW_BLOCK, ROW_BLOCK), ROW_BLOCK)

        def add(c, sums):
            total, squares = sums
            columns = pl.ds(pl.multiple_of(c * chunk, chunk), chunk)
            values = hidden[:, place, columns].reshape(rows, chunk).astype(F32)
            for k in range(0, chunk, lanes):
                squares += values[:, k : k + lanes] * values[:, k : k + lanes]
            gained = values * gain[:, columns]
            high = gained.astype(BF16)
            low = (gained - high.astype(F32)).astype(BF16)
            weights = down[n, :, columns]
            for part in (high, low):
                total += lax.dot_general(
                    part, weights, (((1,), (1,)), ((), ())), preferred_element_type=F32
                )
            return total, squares

        total, squares = lax.fori_loop(
            0, width // chunk, add, (jnp.zeros((rows, rank), F32), jnp.zeros((rows, lanes), F32))
        )
        squares = jnp.sum(squares, axis=1, keepdims=True)
        out[n] = jnp.concatenate([total, jnp.broadcast_to(squares, (rows, rank))], axis=1)


def shrink_kernel(plan, lengths, scales, mine, other, kept, leaving_out, guest_scale):
    first = lax.axis_index("replica") * mine.shape[0]
    adapters, rows, lanes = mine.shape
    rank = lanes // 2
    leaving = jnp.zeros((rows, rank), F32)
    for n in range(adapters):
        total = mine[n] + other[n]
        squares = total[:, rank : rank + 1]
        shrink = total[:, :rank] * lax.rsqrt(squares / MODEL_WIDTH + EPSILON)
        place = lax.broadcasted_iota(jnp.int32, (rows, rank), 0) % ROW_BLOCK
        shrink = jnp.where(place < lengths[first + n], shrink, 0.0)
        removed = plan[LEAVING] == n
        leaving = jnp.where(removed, shrink, leaving)
        kept[n] = jnp.where(removed, 0.0, shrink).astype(BF16)
    leaving_out[...] = leaving.astype(BF16)
    guest = jnp.maximum(plan[SOURCE], 0) * adapters + jnp.maximum(plan[SOURCE_SLOT], 0)
    guest_scale[...] = jnp.full(guest_scale.shape, scales[guest], F32)


def serve(shrink, weights, scale, held, row, out, sems):
    steps = held.shape[0]

    @pl.loop(0, weights.shape[-1] // CHUNK)
    def _(k):
        columns = pl.ds(pl.multiple_of(k * CHUNK, CHUNK), CHUNK)
        delta = jnp.dot(shrink, weights[:, columns], preferred_element_type=F32)
        held[:, :, columns] = (delta * scale).astype(BF16).reshape(steps, ROW_BLOCK, CHUNK)
        served_copy(k, held, row, out, sems).start()


def served_copy(k, held, row, out, sems):
    columns = pl.ds(pl.multiple_of(k * CHUNK, CHUNK), CHUNK)
    rows = pl.ds(pl.multiple_of(row, ROW_BLOCK), ROW_BLOCK)
    return pltpu.make_async_copy(held.at[:, :, columns], out.at[:, rows, columns], sems.at[k])


def resident_kernel(scales, kept, up, out, held, sems):
    first = lax.axis_index("replica") * up.shape[0]

    @pl.loop(0, up.shape[0])
    def _(n):
        serve(kept[n], up.at[n], scales[first + n], held.at[n], n * ROW_BLOCK, out, sems.at[n])

    @pl.loop(0, up.shape[0])
    def _(n):
        @pl.loop(0, up.shape[2] // CHUNK)
        def _(k):
            served_copy(k, held.at[n], n * ROW_BLOCK, out, sems.at[n]).wait()


def guest_kernel(scale, block, shrink, _, out, held, sems):
    row = out.shape[1] - ROW_BLOCK
    serve(shrink[...], block, scale[0, 0], held, row, out, sems)

    @pl.loop(0, block.shape[1] // CHUNK)
    def _(k):
        served_copy(k, held, row, out, sems).wait()


def paired(replicas, hidden, down_weight, up_weight, scales, gain, lengths, moves):
    adapters, rank, width = down_weight.shape
    steps = hidden.shape[0]
    rows = steps * ROW_BLOCK
    shape = jax.ShapeDtypeStruct

    plan, block = pl.pallas_call(
        functools.partial(cut_kernel, replicas),
        out_shape=[pltpu.SMEM((4,), jnp.int32), shape((rank, width), BF16)],
        in_specs=[HBM, HBM],
        out_specs=[SMEM, VMEM],
        scratch_shapes=[
            pltpu.SMEM(moves.shape, jnp.int32),
            pltpu.VMEM(up_weight.shape, BF16),
            pltpu.SemaphoreType.DMA,
            pltpu.SemaphoreType.DMA((adapters, PARTS)),
        ],
        compiler_params=params(),
        cost_estimate=pl.CostEstimate(
            flops=0, bytes_accessed=4 * rank * width, transcendentals=0
        ),
        name="cut",
    )(pltpu.with_memory_space_constraint(moves, pltpu.HBM), up_weight)

    def swap(bits, *upward):
        partners = [(i, i ^ bits) for i in range(replicas)]
        across = [(i, k) for i, k in partners if not upward or (i < k) == upward[0]]

        def branch(block, plan, hidden, down_weight, up_weight, scales, gain, lengths):
            visiting = lax.ppermute(block, "replica", across)
            mine = pl.pallas_call(
                project_kernel,
                out_shape=shape((adapters, rows, 2 * rank), F32),
                in_specs=[VMEM] * 3,
                out_specs=VMEM,
                compiler_params=params(),
                cost_estimate=pl.CostEstimate(
                    flops=4 * adapters * rows * rank * width,
                    bytes_accessed=4 * adapters * rows * width,
                    transcendentals=0,
                ),
                name="project",
            )(hidden, down_weight, gain)
            other = lax.ppermute(mine, "tensor", [(0, 1), (1, 0)])
            kept, leaving, guest_scale = pl.pallas_call(
                shrink_kernel,
                out_shape=[
                    shape((adapters, rows, rank), BF16),
                    shape((rows, rank), BF16),
                    shape((8, 128), F32),
                ],
                in_specs=[SMEM, SMEM, SMEM, VMEM, VMEM],
                out_specs=[VMEM] * 3,
                compiler_params=params(),
                name="shrink",
            )(plan, lengths, scales, mine, other)
            arriving = lax.ppermute(leaving, "replica", partners)
            out_shape = shape((steps, (adapters + 1) * ROW_BLOCK, width), BF16)
            out = pl.pallas_call(
                resident_kernel,
                out_shape=out_shape,
                in_specs=[SMEM, VMEM, VMEM],
                out_specs=HBM,
                scratch_shapes=[
                    pltpu.VMEM((adapters, steps, ROW_BLOCK, width), BF16),
                    pltpu.SemaphoreType.DMA((adapters, width // CHUNK)),
                ],
                compiler_params=params(),
                cost_estimate=pl.CostEstimate(
                    flops=2 * adapters * rows * rank * width,
                    bytes_accessed=4 * adapters * rows * width,
                    transcendentals=0,
                ),
                name="resident",
            )(scales, kept, up_weight)
            return pl.pallas_call(
                guest_kernel,
                out_shape=out_shape,
                in_specs=[VMEM, VMEM, VMEM, HBM],
                out_specs=HBM,
                scratch_shapes=[
                    pltpu.VMEM((steps, ROW_BLOCK, width), BF16),
                    pltpu.SemaphoreType.DMA((width // CHUNK,)),
                ],
                input_output_aliases={3: 0},
                compiler_params=params(),
                cost_estimate=pl.CostEstimate(
                    flops=2 * rows * rank * width,
                    bytes_accessed=2 * (rank + rows) * width,
                    transcendentals=0,
                ),
                name="guest",
            )(guest_scale, visiting, arriving, out)

        return branch

    return lax.switch(
        plan[BRANCH],
        [swap(bits) for bits in range(1, replicas)]
        + [swap(bits, upward) for bits in range(1, replicas) for upward in (True, False)],
        block,
        plan,
        hidden,
        down_weight,
        up_weight,
        scales,
        gain.reshape(1, width),
        lengths,
    )


def summed(hidden, down_weight, up_weight, scales, gain, lengths, moves):
    adapters, rank, width = down_weight.shape
    steps = hidden.shape[0]
    segment = hidden.shape[1] // adapters
    me = lax.axis_index("replica")
    first = me * adapters
    sources, slots, targets = moves[:, 0], moves[:, 1], moves[:, 2]
    here = lax.dynamic_slice_in_dim(lengths, first, adapters)
    alive = jnp.arange(segment, dtype=jnp.int32)[None, :] < here[:, None]
    values = jnp.where(
        alive[None, :, :, None], hidden.reshape(steps, adapters, segment, width), 0
    ).astype(F32)
    squares = lax.psum(jnp.sum(values * values, axis=3), "tensor")
    normed = (values * lax.rsqrt(squares[..., None] / MODEL_WIDTH + EPSILON) * gain).astype(BF16)
    shrink = jnp.einsum("tnsd,nrd->tnsr", normed, down_weight, preferred_element_type=F32)
    shrink = lax.psum(shrink, "tensor").astype(BF16)
    delta = jnp.einsum("tnsr,nrd->tnsd", shrink, up_weight, preferred_element_type=F32)
    scale = lax.dynamic_slice_in_dim(scales, first, adapters)
    served = (delta * scale[None, :, None, None]).astype(BF16)
    leaving = sources == me
    slot = jnp.sum(jnp.where(leaving, slots, 0))
    parcel = lax.dynamic_index_in_dim(served, slot, 1, keepdims=False)
    guest = jnp.zeros_like(parcel)
    for move in range(MOVES):
        arrived = lax.psum(jnp.where(leaving[move], parcel, jnp.zeros_like(parcel)), "replica")
        guest = jnp.where(targets[move] == me, arrived, guest)
    removed = (jnp.arange(adapters) == slot) & jnp.any(leaving)
    served = jnp.where(removed[None, :, None, None], jnp.zeros_like(served), served)
    result = jnp.concatenate([served, guest[:, None]], axis=1)
    return result.reshape(steps, (adapters + 1) * segment, width)


def solution(mesh):
    replicas = mesh.shape["replica"]
    body = functools.partial(paired, replicas) if replicas == 2 * MOVES else summed
    return jax.shard_map(
        body,
        mesh=mesh,
        in_specs=(
            P(None, ("groups", "replica"), "tensor"),
            P("replica", None, "tensor"),
            P("replica", None, "tensor"),
            P(),
            P("tensor"),
            P("groups"),
            P("groups", None),
        ),
        out_specs=P(None, ("groups", "replica"), "tensor"),
        check_vma=False,
    )
```
